256 devices in a mesh: row: 16 (over x_lo, z), col: 16 (over x_hi, y, core).
Axes of the slice: x: 4 (x_hi: 2, x_lo: 2; x = x_hi * 2 + x_lo), y: 4, z: 8, core: 2. Of those that a mesh axis runs over, the one named last changes fastest.
Arguments:
- features: bfloat16 [131072, 256], P(('row', 'col')), may hold values from -6 to 6
- self_weight: bfloat16 [256, 256], replicated, may hold values from -0.375 to 0.375
- neigh_weight: bfloat16 [256, 256], replicated, may hold values from -1.5 to 1.5
- tile_coords: int32 [16, 16, 512, 2], P('row', 'col'), may hold values from 0 to 63, as said below
- tile_columns: int32 [16, 16, 512, 8, 128], P('row', 'col'), may hold values from 0 to 128, as said below
- degree: int32 [131072], P(('row', 'col')), may hold values from 12 to 48
- out_grad: bfloat16 [131072, 256], P(('row', 'col')), may hold values from -6 to 6
Outputs:
- output: bfloat16 [131072, 256], P(('row', 'col'))
- feat_grad: bfloat16 [131072, 256], P(('row', 'col'))
- self_grad: float32 [256, 256], replicated
- neigh_grad: float32 [256, 256], replicated
The draws below stay inside these ranges and needn't reach their ends.
Inputs may be any that keep to these rules, and one draw needn't show every extreme that they name: `tile_coords`: row blocks lie below 4 * 16 and column blocks below 4 * 16. `tile_columns`: entry 128 marks an empty slot. A device's used tiles take its first slots; the remaining slots are all empty; some device uses all 512 slots.
All inputs are finite; a program needn't handle non-finite values.
Results may differ from the reference program's by a relative error of at most 0.0056.
Values may be sent and summed in bfloat16 or wider, within the bound.
A program may use at most 64 MiB of HBM per device.

```python
import jax
import jax.numpy as jnp
from jax import lax

F = 256
TILE = 128
NNZ_ROW = 8
NB_DEV = 4
TILES_DEV = 512
NODES = 131072
N_ROW = 16
N_COL = 16


def draw_tile_coords(key, part):
    key = jax.random.fold_in(key, 1)
    first_key, second_key = jax.random.split(key)
    first = jax.random.randint(first_key, (N_ROW, N_COL, TILES_DEV, 1), 0, NB_DEV * N_COL)
    second = jax.random.randint(second_key, (N_ROW, N_COL, TILES_DEV, 1), 0, NB_DEV * N_ROW)
    return jnp.concatenate([first, second], axis=3).astype(jnp.int32)


def draw_tile_columns(key, part):
    key = jax.random.fold_in(key, 2)
    count_key, busy_key, column_key, keep_key = jax.random.split(key, 4)
    counts = jax.random.randint(count_key, (N_ROW * N_COL,), TILES_DEV // 4, TILES_DEV + 1)
    busiest = jax.random.randint(busy_key, (), 0, N_ROW * N_COL)
    counts = jnp.where(jnp.arange(N_ROW * N_COL, dtype=jnp.int32) == busiest, TILES_DEV, counts)
    counts = counts.reshape(N_ROW, N_COL)
    shape = (N_ROW, N_COL, TILES_DEV, NNZ_ROW, TILE)
    columns = jax.random.randint(column_key, shape, 0, TILE)
    keep = jax.random.randint(keep_key, shape, 0, TILES_DEV * NNZ_ROW) < 48 * NB_DEV
    live = jnp.arange(TILES_DEV, dtype=jnp.int32)[None, None, :] < counts[:, :, None]
    chosen = keep & live[:, :, :, None, None]
    return jnp.where(chosen, columns, TILE).astype(jnp.int32)


def place_ends(array, stream_key, low, top_value):
    shape = array.shape
    place = [jax.random.randint(jax.random.fold_in(stream_key, axis), (), 0, shape[axis]) for axis in range(len(shape))]
    array = array.at[tuple(place)].set(low)
    longest = shape.index(max(shape))
    place[longest] = (place[longest] + 1) % shape[longest]
    return array.at[tuple(place)].set(top_value)


def levels(key, extent, cuts, least, top_value):
    gain, own = 1.0, jax.random.fold_in(key, 6)
    for dim, parts in cuts:
        steps = jnp.exp(jax.random.uniform(jax.random.fold_in(own, dim), (parts,), jnp.float32, least / len(cuts), top_value / len(cuts)))
        gain = gain * jnp.repeat(steps, extent[dim] // parts).reshape([-1 if axis == dim else 1 for axis in range(len(extent))])
    return gain


def noise(stream_key, shape, spread, reach, cuts=(), held_as=jnp.bfloat16):
    values = spread * jax.random.normal(stream_key, shape, jnp.float32)
    if cuts:
        values = values * levels(stream_key, shape, cuts, -0.22, 0.18)
    return jnp.clip(values, -reach, reach).astype(held_as)


def setup_inputs(seed: int = 0) -> dict:
    arg_keys = jax.random.split(jax.random.key(seed), 8)
    features = noise(arg_keys[0], (NODES, F), 1.0, 6.0, ((0, 256),))
    self_weight = noise(arg_keys[1], (F, F), F ** -0.5, 0.375)
    neigh_weight = noise(arg_keys[2], (F, F), (F // 16) ** -0.5, 1.5)
    tile_coords = draw_tile_coords(jax.random.fold_in(arg_keys[7], 71), 0)
    tile_columns = draw_tile_columns(jax.random.fold_in(arg_keys[7], 71), 0)
    degree = place_ends(jax.random.randint(arg_keys[5], (NODES,), 12, 49), jax.random.fold_in(arg_keys[5], 1), 12, 48).astype(jnp.int32)
    out_grad = noise(arg_keys[6], (NODES, F), 1.0, 6.0, ((0, 256),))
    return {"features": features, "self_weight": self_weight, "neigh_weight": neigh_weight, "tile_coords": tile_coords, "tile_columns": tile_columns, "degree": degree, "out_grad": out_grad}


def edge_lists(row_index, col_index, coord_slots, column_slots):
    row_blocks = NB_DEV * N_COL
    first = coord_slots[:, 0]
    second = coord_slots[:, 1]
    lanes = jnp.arange(TILE, dtype=jnp.int32)
    target = (row_index * row_blocks + first) * TILE
    target = target[:, None, None] + lanes[None, None, :] + jnp.zeros_like(column_slots)
    global_block = ((second // NB_DEV) * N_COL + col_index) * NB_DEV + second % NB_DEV
    source = global_block[:, None, None] * TILE + jnp.minimum(column_slots, TILE - 1)
    valid = (column_slots < TILE).astype(jnp.float32)
    return target.reshape(-1), source.reshape(-1), valid.reshape(-1)


def reference(features, self_weight, neigh_weight, tile_coords, tile_columns, degree, out_grad):
    devices_all = N_ROW * N_COL
    row_ids = jnp.repeat(jnp.arange(N_ROW, dtype=jnp.int32), N_COL)
    col_ids = jnp.tile(jnp.arange(N_COL, dtype=jnp.int32), N_ROW)
    coords = tile_coords.reshape(devices_all, TILES_DEV, 2)
    columns = tile_columns.reshape(devices_all, TILES_DEV, NNZ_ROW, TILE)
    features_wide = features.astype(jnp.float32)

    def forward_step(running, inputs):
        row_index, col_index, coord_slots, column_slots = inputs
        target, source, valid = edge_lists(row_index, col_index, coord_slots, column_slots)
        values = features_wide[source] * valid[:, None]
        return running.at[target].add(values), None

    summed, _ = lax.scan(forward_step, jnp.zeros((NODES, F), jnp.float32), (row_ids, col_ids, coords, columns))
    divisor = degree.astype(jnp.float32)[:, None]
    mean_feat = (summed / divisor).astype(jnp.bfloat16)
    pre = jnp.dot(features, self_weight, preferred_element_type=jnp.float32) + jnp.dot(mean_feat, neigh_weight, preferred_element_type=jnp.float32)
    sigma = jax.nn.sigmoid(pre)
    output = (pre * sigma).astype(jnp.bfloat16)
    g_pre = (out_grad.astype(jnp.float32) * sigma * (1.0 + pre * (1.0 - sigma))).astype(jnp.bfloat16)
    self_grad = jnp.dot(features.T, g_pre, preferred_element_type=jnp.float32)
    neigh_grad = jnp.dot(mean_feat.T, g_pre, preferred_element_type=jnp.float32)
    scaled = (jnp.dot(g_pre, neigh_weight.T, preferred_element_type=jnp.float32) / divisor).astype(jnp.bfloat16)
    scaled_wide = scaled.astype(jnp.float32)

    def backward_step(running, inputs):
        row_index, col_index, coord_slots, column_slots = inputs
        target, source, valid = edge_lists(row_index, col_index, coord_slots, column_slots)
        values = scaled_wide[target] * valid[:, None]
        return running.at[source].add(values), None

    back_sum, _ = lax.scan(backward_step, jnp.zeros((NODES, F), jnp.float32), (row_ids, col_ids, coords, columns))
    feat_grad = (jnp.dot(g_pre, self_weight.T, preferred_element_type=jnp.float32) + back_sum).astype(jnp.bfloat16)
    return output, feat_grad, self_grad, neigh_grad
```

```python
import jax
import jax.numpy as jnp
from jax import lax
from jax.experimental import pallas as pl
from jax.experimental.pallas import tpu as pltpu
from jax.sharding import PartitionSpec as P

TILES = 512
GROUP = 4
GROUPS = 176
LANES = 768
BF = jnp.bfloat16
F32 = jnp.float32


def iota(shape, dim):
    return lax.broadcasted_iota(jnp.int32, shape, dim)


def mask_bf16(mask):
    return mask.astype(F32).astype(BF)


def order_kernel(coords_ref, coords_t_ref, out_ref):
    for d in range(2):
        key = coords_ref[:, d : d + 1]
        hot = (key == iota((TILES, 128), 1)).astype(F32)
        earlier = mask_bf16(iota((TILES, TILES), 0) > iota((TILES, TILES), 1))
        rank = jnp.dot(earlier, hot.astype(BF), preferred_element_type=F32)
        count = jnp.sum(hot, axis=0, keepdims=True)
        groups = (count.astype(jnp.int32) + (GROUP - 1)) >> 2
        upper = mask_bf16(iota((128, 128), 0) < iota((128, 128), 1))
        wide = jnp.broadcast_to(groups.astype(F32), (8, 128)).astype(BF)
        start = jnp.dot(wide, upper, preferred_element_type=F32)[0:1]
        place = jnp.sum(hot * (GROUP * start + rank), axis=1, keepdims=True).astype(jnp.int32)
        slot = mask_bf16(place == iota((TILES, LANES), 1))
        t, r = iota((8, TILES), 1), iota((8, TILES), 0)
        own, other = coords_t_ref[d : d + 1, :], coords_t_ref[1 - d : 2 - d, :]
        rows = jnp.where(
            r == 0, t >> 4, jnp.where(r == 1, t & 15, jnp.where(r == 2, own, jnp.where(r == 3, other, 1)))
        )
        got = jnp.dot(rows.astype(F32).astype(BF), slot, preferred_element_type=F32).astype(jnp.int32)
        out_ref[d, 0:1, :] = jnp.where(got[4:5] > 0, got[0:1] * 16 + got[1:2], TILES)
        out_ref[d, 1:2, :] = got[2:3]
        out_ref[d, 2:3, :] = got[3:4]
        out_ref[d, 3:4, 0:128] = jnp.where(groups > 0, start.astype(jnp.int32) + groups - 1, GROUPS)
        out_ref[d, 3:4, 128:LANES] = jnp.zeros((1, LANES - 128), jnp.int32)
        out_ref[d, 4:8, :] = jnp.zeros((4, LANES), jnp.int32)


class Net:
    def __init__(self, send, recv):
        self.send, self.recv, self.ids, self.open = send, recv, {}, []

    def put(self, name, src, dst, device):
        n = self.ids.setdefault(name, len(self.ids))
        copy = pltpu.make_async_remote_copy(
            src_ref=src,
            dst_ref=dst,
            send_sem=self.send.at[n],
            recv_sem=self.recv.at[n],
            device_id=device,
            device_id_type=pl.DeviceIdType.MESH,
        )
        copy.start()
        self.open.append(copy)

    def wait(self, name, dst, device):
        n = self.ids[name]
        pltpu.make_async_remote_copy(
            src_ref=dst,
            dst_ref=dst,
            send_sem=self.send.at[n],
            recv_sem=self.recv.at[n],
            device_id=device,
            device_id_type=pl.DeviceIdType.MESH,
        ).wait_recv()

    def finish(self):
        for copy in self.open:
            copy.wait_send()


N_SEMS = 280


def main_kernel(
    tab, x_ref, sw_ref, nw_ref, cols_ref, deg_ref, og_ref,
    out_ref, fg_ref, sg_ref, ng_ref,
    at, src0, src1, s0, s1, acc, b0, b1, mean_t, g_ref,
    snd1, rcv1, r_py, r_px, r_qx, r_qy,
    t_xa, r_xa, r_z, t_z, t_xb, r_xb,
    w_sum, w_r1, w_2, w_3,
    send, recv,
):
    r, c = lax.axis_index("row"), lax.axis_index("col")
    xl, z = lax.div(r, 8), lax.rem(r, 8)
    core, chip = lax.rem(c, 2), lax.div(c, 2)
    y, xh = lax.rem(chip, 4), lax.div(chip, 4)
    src, s, b = (src0, src1), (s0, s1), (b0, b1)
    net = Net(send, recv)

    def row_of(dx, dz):
        return lax.rem(xl + dx, 2) * 8 + lax.rem(z + (dz + 8), 8)

    def col_of(dx, dy, dc=0):
        return (lax.rem(xh + dx, 2) * 4 + lax.rem(y + dy, 4)) * 2 + lax.rem(core + dc, 2)

    def to_row(dx, dz):
        return {"row": row_of(dx, dz)}

    def to_col(dx, dy, dc=0):
        return {"col": col_of(dx, dy, dc)}

    barrier = pltpu.get_barrier_semaphore()

    def greet(d, _):
        pl.semaphore_signal(
            barrier, inc=1, device_id={"row": lax.rem(r + d, 16)}, device_id_type=pl.DeviceIdType.MESH
        )
        pl.semaphore_signal(
            barrier, inc=1, device_id={"col": lax.rem(c + d, 16)}, device_id_type=pl.DeviceIdType.MESH
        )
        return 0

    lax.fori_loop(1, 16, greet, 0)

    for k in range(4):
        turned = x_ref[128 * k : 128 * k + 128, :].astype(F32).T.astype(BF)
        src0[4 * r + k] = turned[0:128]
        src1[4 * r + k] = turned[128:256]
    for h in range(2):
        s[h][GROUPS] = jnp.zeros((128, 128), BF)
    at[TILES] = jnp.zeros((128, 128), BF)
    acc[...] = jnp.zeros((128, 128), F32)
    pl.semaphore_wait(barrier, 30)

    def block(h, q, dx, dz):
        return src[h].at[pl.ds(4 * row_of(dx, dz) + 2 * q, 2)]

    streams = ((1, 0), (0, 0), (0, 1))

    def hops(h, q, dx):
        return (4, 3) if (h + q + dx) % 2 else (3, 4)

    def ring_send(h, q, dx, step, way):
        if step <= hops(h, q, dx)[way]:
            sign = 1 - 2 * way
            ref = block(h, q, dx, -sign * (step - 1))
            net.put(("ring", h, q, dx, step, way), ref, ref, to_row(0, sign))

    def gather_start(h):
        ref = block(h, 0, 0, 0)
        net.put(("x0", h), ref, ref, to_row(1, 0))
        for way in range(2):
            ring_send(h, 1, 0, 1, way)
        ref = block(h, 1, 0, 0)
        net.put(("x1", h, 0), ref, ref, to_row(1, 0))
        for way in range(2):
            ring_send(h, 0, 0, 1, way)

    def gather_mid(h):
        net.wait(("x0", h), block(h, 0, 1, 0), to_row(1, 0))
        for way in range(2):
            ring_send(h, 0, 1, 1, way)

    def gather_step(h, step):
        for q, dx in streams:
            for way in range(2):
                if step <= hops(h, q, dx)[way]:
                    sign = 1 - 2 * way
                    ref = block(h, q, dx, -sign * step)
                    net.wait(("ring", h, q, dx, step, way), ref, to_row(0, -sign))
                    ring_send(h, q, dx, step + 1, way)
                    if q == 1:
                        net.put(("x1", h, -sign * step), ref, ref, to_row(1, 0))

    def gather_end(h):
        plus, minus = hops(h, 1, 0)
        for dz in range(-plus, minus + 1):
            net.wait(("x1", h, dz), block(h, 1, 1, dz), to_row(1, 0))

    def build(lo, hi):
        def body(t, _):
            slots = cols_ref[t]
            lane = iota((128, 128), 0).astype(jnp.int16)
            total = None
            for n in range(8):
                hit = jnp.broadcast_to(slots[n : n + 1, :], (128, 128)).astype(jnp.int16) == lane
                one = jnp.where(hit, jnp.ones((), BF), jnp.zeros((), BF))
                total = one if total is None else total + one
            at[t] = total
            return 0

        lax.fori_loop(lo, hi, body, 0, unroll=4)

    def multiply(d, h, lo, hi):
        def body(p, last):
            tiles = [at[tab[d, 0, GROUP * p + i]] for i in range(GROUP)]
            sources = [(src, b)[d][h][tab[d, 2, GROUP * p + i]] for i in range(GROUP)]
            key = tab[d, 1, GROUP * p]
            if d == 0:
                left, right = jnp.concatenate(sources, axis=1), jnp.concatenate(tiles, axis=0)
            else:
                left, right = jnp.concatenate(tiles, axis=1), jnp.concatenate(sources, axis=0)
            product = jnp.dot(left, right, preferred_element_type=F32)
            total = jnp.where(key == last, acc[...], 0.0) + product
            acc[...] = total
            s[h][p] = total.astype(BF)
            return key

        first = tab[d, 1, GROUP * (lo - 1)] if lo else jnp.int32(-1)
        lax.fori_loop(lo, hi, body, first, unroll=16)

    def part(d, h, block_id):
        return s[h][tab[d, 3, block_id]].astype(F32)

    def cols_start(h):
        for dx in (1, 0):
            for dy in (1, 3, 2, 0):
                j = dx * 4 + dy
                for k in range(4):
                    snd1[h, j, k] = s[h][tab[0, 3, 4 * col_of(dx, dy, 1) + k]]
                net.put(("core", h, j), snd1.at[h, j], rcv1.at[h, j], to_col(0, 0, 1))

    def cols_second(h):
        for dx in (1, 0):
            for dy in (1, 3, 2, 0):
                j = dx * 4 + dy
                net.wait(("core", h, j), rcv1.at[h, j], to_col(0, 0, 1))
                for k in range(4):
                    rcv1[h, j, k] = (part(0, h, 4 * col_of(dx, dy) + k) + rcv1[h, j, k].astype(F32)).astype(BF)
                if dx == 1:
                    net.put(("qx", h, dy), rcv1.at[h, j, pl.ds(2, 2)], r_qx.at[h, dy], to_col(1, 0))
                if dy:
                    net.put(("py", h, dy, dx), rcv1.at[h, j, pl.ds(0, 2)], r_py.at[h, dy - 1, dx], to_col(0, dy))

    def cols_third(h):
        for dy in (1, 3, 2):
            net.wait(("qx", h, dy), r_qx.at[h, dy], to_col(1, 0))
            r_qx[h, dy] = (rcv1[h, dy, 2:4].astype(F32) + r_qx[h, dy].astype(F32)).astype(BF)
            net.put(("qy", h, dy), r_qx.at[h, dy], r_qy.at[h, dy - 1], to_col(0, dy))
        total = rcv1[h, 4, 0:2].astype(F32)
        for dy in (1, 3, 2):
            net.wait(("py", h, dy, 1), r_py.at[h, dy - 1, 1], to_col(0, 4 - dy))
            total = total + r_py[h, dy - 1, 1].astype(F32)
        snd1[h, 8, 0:2] = total.astype(BF)
        net.put(("px", h), snd1.at[h, 8, pl.ds(0, 2)], r_px.at[h], to_col(1, 0))

    def cols_end(h):
        total = rcv1[h, 0, 0:2].astype(F32)
        for dy in (1, 3, 2):
            net.wait(("py", h, dy, 0), r_py.at[h, dy - 1, 0], to_col(0, 4 - dy))
            total = total + r_py[h, dy - 1, 0].astype(F32)
        net.wait(("px", h), r_px.at[h], to_col(1, 0))
        total = total + r_px[h].astype(F32)
        net.wait(("qx", h, 0), r_qx.at[h, 0], to_col(1, 0))
        second = rcv1[h, 0, 2:4].astype(F32) + r_qx[h, 0].astype(F32)
        for dy in (1, 3, 2):
            net.wait(("qy", h, dy), r_qy.at[h, dy - 1], to_col(0, 4 - dy))
            second = second + r_qy[h, dy - 1].astype(F32)
        for k in range(4):
            value = (total if k < 2 else second)[k % 2]
            mean_t[k, 128 * h : 128 * h + 128, :] = (value / deg_ref[k : k + 1, :].astype(F32)).astype(BF)

    turned_dims = (((1,), (1,)), ((), ()))

    def dense():
        for k in range(4):
            rows = slice(128 * k, 128 * k + 128)
            mean = mean_t[k].astype(F32).T.astype(BF)
            pre = jnp.dot(x_ref[rows, :], sw_ref[...], preferred_element_type=F32)
            pre = pre + jnp.dot(mean, nw_ref[...], preferred_element_type=F32)
            sig = jax.nn.sigmoid(pre)
            out_ref[rows, :] = (pre * sig).astype(BF)
            g = (og_ref[rows, :].astype(F32) * sig * (1.0 + pre * (1.0 - sig))).astype(BF)
            g_ref[k] = g
            d_mean = lax.dot_general(g, nw_ref[...], turned_dims, preferred_element_type=F32)
            divisor = jnp.broadcast_to(deg_ref[k : k + 1, :].astype(F32), (128, 128)).T
            b0[4 * c + k] = (d_mean[:, 0:128] / divisor).astype(BF)
            b1[4 * c + k] = (d_mean[:, 128:256] / divisor).astype(BF)

    def cblock(h, q, dx, dy, dc=0):
        return b[h].at[pl.ds(4 * col_of(dx, dy, dc) + 2 * q, 2)]

    def to_core(h, q, dx, dy):
        ref = cblock(h, q, dx, dy)
        net.put(("bc", h, q, dx, dy), ref, ref, to_col(0, 0, 1))

    def back_start(h):
        ref = cblock(h, 0, 0, 0)
        net.put(("bx0", h), ref, ref, to_col(1, 0))
        ref = cblock(h, 1, 0, 0)
        for dy in (1, 3, 2):
            net.put(("by1", h, dy), ref, ref, to_col(0, dy))
        net.put(("bx1", h, 0), ref, ref, to_col(1, 0))
        ref = cblock(h, 0, 0, 0)
        for dy in (1, 3, 2):
            net.put(("by0", h, 0, dy), ref, ref, to_col(0, dy))
        to_core(h, 0, 0, 0)
        to_core(h, 1, 0, 0)

    def back_mid(h):
        ref = cblock(h, 0, 1, 0)
        net.wait(("bx0", h), ref, to_col(1, 0))
        for dy in (1, 3, 2):
            net.put(("by0", h, 1, dy), ref, ref, to_col(0, dy))
        for dy in (1, 3, 2):
            ref = cblock(h, 1, 0, 4 - dy)
            net.wait(("by1", h, dy), ref, to_col(0, 4 - dy))
            net.put(("bx1", h, dy), ref, ref, to_col(1, 0))
        to_core(h, 0, 1, 0)
        for dy in (1, 3, 2):
            to_core(h, 1, 0, 4 - dy)

    def back_late(h):
        for dy in (1, 3, 2):
            net.wait(("by0", h, 0, dy), cblock(h, 0, 0, 4 - dy), to_col(0, 4 - dy))
            to_core(h, 0, 0, 4 - dy)
        for dy in (0, 1, 3, 2):
            net.wait(("bx1", h, dy), cblock(h, 1, 1, (4 - dy) % 4), to_col(1, 0))
            to_core(h, 1, 1, (4 - dy) % 4)
        for dy in (1, 3, 2):
            net.wait(("by0", h, 1, dy), cblock(h, 0, 1, 4 - dy), to_col(0, 4 - dy))
            to_core(h, 0, 1, 4 - dy)

    def back_end(h):
        for q in range(2):
            for dx in range(2):
                for dy in range(4):
                    net.wait(("bc", h, q, dx, dy), cblock(h, q, dx, dy, 1), to_col(0, 0, 1))

    def rows_start(h):
        for dz in (4, 3, 5, 2, 6, 1, 7, 0):
            for k in range(2):
                t_xa[h, dz, k] = s[h][tab[1, 3, 4 * row_of(1, dz) + 2 + k]]
            net.put(("xa", h, dz), t_xa.at[h, dz], r_xa.at[h, dz], to_row(1, 0))
        for n, (q, dx) in enumerate(streams):
            if q == 0:
                rows_first(h, n)

    def term(h, n, dz):
        q, dx = streams[n]
        dz = dz % 8
        value = [part(1, h, 4 * row_of(dx, dz) + 2 * q + k) for k in range(2)]
        if q == 1:
            value = [value[k] + r_xa[h, dz, k].astype(F32) for k in range(2)]
        return value

    def rows_first(h, n):
        for way in range(2):
            sign = 1 - 2 * way
            far = hops(h, *streams[n])[way]
            if streams[n][0] == 1:
                net.wait(("xa", h, sign * far % 8), r_xa.at[h, sign * far % 8], to_row(1, 0))
            value = term(h, n, sign * far)
            for k in range(2):
                t_z[h, n, way, k] = value[k].astype(BF)
            net.put(("z", h, n, way, 1), t_z.at[h, n, way], r_z.at[h, n, way, 0], to_row(0, sign))

    def rows_second(h):
        rows_first(h, 0)

    def rows_step(h, step):
        for n in (1, 2, 0):
            for way in range(2):
                sign = 1 - 2 * way
                far = hops(h, *streams[n])[way]
                if step >= far:
                    continue
                dz = sign * (far - step)
                if streams[n][0] == 1:
                    net.wait(("xa", h, dz % 8), r_xa.at[h, dz % 8], to_row(1, 0))
                value = term(h, n, dz)
                ref = r_z.at[h, n, way, step - 1]
                net.wait(("z", h, n, way, step), ref, to_row(0, -sign))
                for k in range(2):
                    r_z[h, n, way, step - 1, k] = (
                        value[k] + r_z[h, n, way, step - 1, k].astype(F32)
                    ).astype(BF)
                net.put(("z", h, n, way, step + 1), ref, r_z.at[h, n, way, step], to_row(0, sign))

    def rows_sum(h, n):
        if streams[n][0] == 1:
            net.wait(("xa", h, 0), r_xa.at[h, 0], to_row(1, 0))
        value = term(h, n, 0)
        for way in range(2):
            far = hops(h, *streams[n])[way]
            net.wait(("z", h, n, way, far), r_z.at[h, n, way, far - 1], to_row(0, 2 * way - 1))
            value = [value[k] + r_z[h, n, way, far - 1, k].astype(F32) for k in range(2)]
        return value

    def rows_late(h):
        value = rows_sum(h, 2)
        for k in range(2):
            t_xb[h, k] = value[k].astype(BF)
        net.put(("xb", h), t_xb.at[h], r_xb.at[h], to_row(1, 0))

    def own_term(k, h):
        return lax.dot_general(
            g_ref[k], sw_ref[128 * h : 128 * h + 128, :], turned_dims, preferred_element_type=F32
        )

    def rows_end(h):
        lanes = slice(128 * h, 128 * h + 128)
        value = rows_sum(h, 0)
        for k in range(2):
            fg_ref[128 * (k + 2) : 128 * (k + 3), lanes] = (value[k] + own_term(k + 2, h)).astype(BF)
        value = rows_sum(h, 1)
        net.wait(("xb", h), r_xb.at[h], to_row(1, 0))
        for k in range(2):
            back = value[k] + r_xb[h, k].astype(F32)
            fg_ref[128 * k : 128 * (k + 1), lanes] = (back + own_term(k, h)).astype(BF)

    def weights_start():
        for h in range(2):
            rows = slice(128 * h, 128 * h + 128)
            own = jnp.concatenate([src[h][4 * r + k] for k in range(4)], axis=1)
            mean = jnp.concatenate([mean_t[k, rows, :] for k in range(4)], axis=1)
            g = jnp.concatenate([g_ref[k] for k in range(4)], axis=0)
            first = jnp.dot(own, g, preferred_element_type=F32).reshape(4, 32, 256)
            second = jnp.dot(mean, g, preferred_element_type=F32).reshape(4, 32, 256)
            w_sum[4 * h : 4 * h + 4] = first
            w_sum[8 + 4 * h : 12 + 4 * h] = second
        for d in range(1, 16):
            target = lax.rem(c + d, 16)
            net.put(("w1", d), w_sum.at[target], w_r1.at[d - 1], {"col": target})

    def weights_second():
        total = w_sum[c]
        for d in range(1, 16):
            net.wait(("w1", d), w_r1.at[d - 1], {"col": lax.rem(c + (16 - d), 16)})
            total = total + w_r1[d - 1]
        w_2[r] = total
        for d in range(1, 16):
            net.put(("w2", d), w_2.at[r], w_2.at[r], {"row": lax.rem(r + d, 16)})

    def weights_third():
        for d in range(1, 16):
            source = lax.rem(r + (16 - d), 16)
            net.wait(("w2", d), w_2.at[source], {"row": source})
        total = w_2[0]
        for n in range(1, 16):
            total = total + w_2[n]
        w_3[c] = total
        for d in range(1, 16):
            net.put(("w3", d), w_3.at[c], w_3.at[c], {"col": lax.rem(c + d, 16)})

    def weights_end():
        for d in range(1, 16):
            source = lax.rem(c + (16 - d), 16)
            net.wait(("w3", d), w_3.at[source], {"col": source})
        for n in range(8):
            sg_ref[32 * n : 32 * n + 32, :] = w_3[n]
            ng_ref[32 * n : 32 * n + 32, :] = w_3[8 + n]

    gather_start(0)
    build(0, 64)
    gather_mid(0)
    build(64, 128)
    gather_step(0, 1)
    gather_start(1)
    build(128, 192)
    gather_step(0, 2)
    gather_mid(1)
    build(192, 288)
    gather_step(0, 3)
    build(288, 384)
    gather_step(0, 4)
    gather_step(1, 1)
    build(384, 512)
    gather_end(0)
    multiply(0, 0, 0, 48)
    gather_step(1, 2)
    multiply(0, 0, 48, 112)
    gather_step(1, 3)
    multiply(0, 0, 112, 176)
    gather_step(1, 4)
    cols_start(0)
    gather_end(1)
    multiply(0, 1, 0, 64)
    cols_second(0)
    multiply(0, 1, 64, 128)
    cols_third(0)
    multiply(0, 1, 128, 176)
    cols_start(1)
    cols_end(0)
    cols_second(1)
    cols_third(1)
    cols_end(1)
    dense()
    back_start(0)
    back_start(1)
    weights_start()
    back_mid(0)
    back_late(0)
    back_mid(1)
    back_end(0)
    multiply(1, 0, 0, 80)
    back_late(1)
    multiply(1, 0, 80, 176)
    rows_start(0)
    weights_second()
    back_end(1)
    rows_second(0)
    multiply(1, 1, 0, 48)
    rows_step(0, 1)
    multiply(1, 1, 48, 96)
    rows_step(0, 2)
    multiply(1, 1, 96, 144)
    rows_step(0, 3)
    multiply(1, 1, 144, 176)
    rows_start(1)
    rows_second(1)
    rows_late(0)
    weights_third()
    rows_step(1, 1)
    rows_step(1, 2)
    rows_end(0)
    rows_step(1, 3)
    weights_end()
    rows_late(1)
    rows_end(1)
    net.finish()


def shards(features, self_weight, neigh_weight, tile_coords, tile_columns, degree, out_grad):
    coords = tile_coords.reshape(TILES, 2)
    tab = pl.pallas_call(order_kernel, out_shape=jax.ShapeDtypeStruct((2, 8, LANES), jnp.int32))(coords, coords.T)
    vmem = pl.BlockSpec(memory_space=pltpu.VMEM)
    shape = jax.ShapeDtypeStruct
    return pl.pallas_call(
        main_kernel,
        out_shape=(shape((512, 256), BF), shape((512, 256), BF), shape((256, 256), F32), shape((256, 256), F32)),
        in_specs=[pl.BlockSpec(memory_space=pltpu.SMEM)] + [vmem] * 6,
        out_specs=[vmem] * 4,
        scratch_shapes=[
            pltpu.VMEM((TILES + 1, 128, 128), BF),
            pltpu.VMEM((64, 128, 128), BF),
            pltpu.VMEM((64, 128, 128), BF),
            pltpu.VMEM((GROUPS + 1, 128, 128), BF),
            pltpu.VMEM((GROUPS + 1, 128, 128), BF),
            pltpu.VMEM((128, 128), F32),
            pltpu.VMEM((64, 128, 128), BF),
            pltpu.VMEM((64, 128, 128), BF),
            pltpu.VMEM((4, 256, 128), BF),
            pltpu.VMEM((4, 128, 256), BF),
            pltpu.VMEM((2, 9, 4, 128, 128), BF),
            pltpu.VMEM((2, 8, 4, 128, 128), BF),
            pltpu.VMEM((2, 3, 2, 2, 128, 128), BF),
            pltpu.VMEM((2, 2, 128, 128), BF),
            pltpu.VMEM((2, 4, 2, 128, 128), BF),
            pltpu.VMEM((2, 3, 2, 128, 128), BF),
            pltpu.VMEM((2, 8, 2, 128, 128), BF),
            pltpu.VMEM((2, 8, 2, 128, 128), BF),
            pltpu.VMEM((2, 3, 2, 4, 2, 128, 128), BF),
            pltpu.VMEM((2, 3, 2, 2, 128, 128), BF),
            pltpu.VMEM((2, 2, 128, 128), BF),
            pltpu.VMEM((2, 2, 128, 128), BF),
            pltpu.VMEM((16, 32, 256), F32),
            pltpu.VMEM((15, 32, 256), F32),
            pltpu.VMEM((16, 32, 256), F32),
            pltpu.VMEM((16, 32, 256), F32),
            pltpu.SemaphoreType.DMA((N_SEMS,)),
            pltpu.SemaphoreType.DMA((N_SEMS,)),
        ],
        compiler_params=pltpu.CompilerParams(
            collective_id=0, has_side_effects=True, vmem_limit_bytes=60 * 1024 * 1024
        ),
    )(
        tab,
        features,
        self_weight,
        neigh_weight,
        tile_columns.reshape(TILES, 8, 128),
        degree.reshape(4, 128),
        out_grad,
    )


def solution(mesh):
    return jax.shard_map(
        shards,
        mesh=mesh,
        in_specs=(
            P(("row", "col"), None),
            P(),
            P(),
            P("row", "col", None, None),
            P("row", "col", None, None, None),
            P(("row", "col")),
            P(("row", "col"), None),
        ),
        out_specs=(P(("row", "col"), None), P(("row", "col"), None), P(), P()),
        check_vma=False,
    )
```

```python
import jax
import jax.numpy as jnp
from jax import lax
from jax.experimental import pallas as pl
from jax.experimental.pallas import tpu as pltpu
from jax.sharding import PartitionSpec as P

TILES = 512
GROUP = 4
GROUPS = 176
LANES = 768
BF = jnp.bfloat16
F32 = jnp.float32


def iota(shape, dim):
    return lax.broadcasted_iota(jnp.int32, shape, dim)


def mask_bf16(mask):
    return mask.astype(F32).astype(BF)


def order_tiles(coords_ref, out_ref):
    own_lane = iota((TILES, TILES), 0) == iota((TILES, TILES), 1)
    earlier = mask_bf16(iota((TILES, TILES), 0) > iota((TILES, TILES), 1))
    upper = mask_bf16(iota((128, 128), 0) < iota((128, 128), 1))
    t, r = iota((8, TILES), 1), iota((8, TILES), 0)
    for d in range(2):
        own, other = coords_ref[d : d + 1, :], coords_ref[1 - d : 2 - d, :]
        key = jnp.sum(jnp.where(own_lane, own.astype(F32), 0.0), axis=1, keepdims=True).astype(jnp.int32)
        hot = (key == iota((TILES, 128), 1)).astype(F32)
        rank = jnp.dot(earlier, hot.astype(BF), preferred_element_type=F32)
        count = jnp.sum(hot, axis=0, keepdims=True)
        groups = (count.astype(jnp.int32) + (GROUP - 1)) >> 2
        wide = jnp.broadcast_to(groups.astype(F32), (8, 128)).astype(BF)
        start = jnp.dot(wide, upper, preferred_element_type=F32)[0:1]
        place = jnp.sum(hot * (GROUP * start + rank), axis=1, keepdims=True).astype(jnp.int32)
        slot = mask_bf16(place == iota((TILES, LANES), 1))
        rows = jnp.where(
            r == 0, t >> 4, jnp.where(r == 1, t & 15, jnp.where(r == 2, own, jnp.where(r == 3, other, 1)))
        )
        got = jnp.dot(rows.astype(F32).astype(BF), slot, preferred_element_type=F32).astype(jnp.int32)
        out_ref[d, 0:1, :] = jnp.where(got[4:5] > 0, got[0:1] * 16 + got[1:2], TILES)
        out_ref[d, 1:2, :] = got[2:3]
        out_ref[d, 2:3, :] = got[3:4]
        out_ref[d, 3:4, 0:128] = jnp.where(groups > 0, start.astype(jnp.int32) + groups - 1, GROUPS)
        out_ref[d, 3:4, 128:LANES] = jnp.zeros((1, LANES - 128), jnp.int32)
        out_ref[d, 4:8, :] = jnp.zeros((4, LANES), jnp.int32)


class Net:
    def __init__(self, send, recv):
        self.send, self.recv, self.ids, self.open = send, recv, {}, []

    def put(self, name, src, dst, device):
        n = self.ids.setdefault(name, len(self.ids))
        copy = pltpu.make_async_remote_copy(
            src_ref=src,
            dst_ref=dst,
            send_sem=self.send.at[n],
            recv_sem=self.recv.at[n],
            device_id=device,
            device_id_type=pl.DeviceIdType.MESH,
        )
        copy.start()
        self.open.append(copy)

    def wait(self, name, dst, device):
        n = self.ids[name]
        pltpu.make_async_remote_copy(
            src_ref=dst,
            dst_ref=dst,
            send_sem=self.send.at[n],
            recv_sem=self.recv.at[n],
            device_id=device,
            device_id_type=pl.DeviceIdType.MESH,
        ).wait_recv()

    def finish(self):
        for copy in self.open:
            copy.wait_send()


N_SEMS = 280


def main_kernel(
    tab, x_ref, sw_ref, nw_ref, cols_hbm, deg_ref, og_ref,
    out_ref, fg_ref, sg_ref, ng_ref,
    at, src0, src1, s0, s1, acc, b0, b1, mean_t, g_ref,
    snd1, rcv1, r_py, r_px, r_qx, r_qy,
    t_xa, r_xa, r_z, t_z, t_xb, r_xb,
    w_sum, w_col, w_part, w_row, w_z, w_all,
    cols_ref, local, send, recv,
):
    r, c = lax.axis_index("row"), lax.axis_index("col")
    xl, z = lax.div(r, 8), lax.rem(r, 8)
    core, chip = lax.rem(c, 2), lax.div(c, 2)
    y, xh = lax.rem(chip, 4), lax.div(chip, 4)
    src, s, b = (src0, src1), (s0, s1), (b0, b1)
    net = Net(send, recv)

    def row_of(dx, dz):
        return lax.rem(xl + dx, 2) * 8 + lax.rem(z + (dz + 8), 8)

    def col_of(dx, dy, dc=0):
        return (lax.rem(xh + dx, 2) * 4 + lax.rem(y + dy, 4)) * 2 + lax.rem(core + dc, 2)

    def to_row(dx, dz):
        return {"row": row_of(dx, dz)}

    def to_col(dx, dy, dc=0):
        return {"col": col_of(dx, dy, dc)}

    barrier = pltpu.get_barrier_semaphore()

    partners = [{"row": lax.rem(r + d, 16)} for d in range(1, 16)]
    partners += [{"col": lax.rem(c + d, 16)} for d in range(1, 16)]
    for partner in partners:
        pl.semaphore_signal(barrier, inc=1, device_id=partner, device_id_type=pl.DeviceIdType.MESH)
    load_cols = pltpu.make_async_copy(cols_hbm, cols_ref, local.at[0])
    load_cols.start()

    for k in range(4):
        turned = x_ref[128 * k : 128 * k + 128, :].astype(F32).T.astype(BF)
        src0[4 * r + k] = turned[0:128]
        src1[4 * r + k] = turned[128:256]
    for h in range(2):
        s[h][GROUPS] = jnp.zeros((128, 128), BF)
    at[TILES] = jnp.zeros((128, 128), BF)
    acc[...] = jnp.zeros((128, 128), F32)
    pl.semaphore_wait(barrier, len(partners))

    def block(h, q, dx, dz):
        return src[h].at[pl.ds(4 * row_of(dx, dz) + 2 * q, 2)]

    streams = ((1, 0), (0, 0), (0, 1))

    def hops(h, q, dx):
        return (4, 3) if (h + q + dx) % 2 else (3, 4)

    def ring_send(h, q, dx, step, way):
        if step <= hops(h, q, dx)[way]:
            sign = 1 - 2 * way
            ref = block(h, q, dx, -sign * (step - 1))
            net.put(("ring", h, q, dx, step, way), ref, ref, to_row(0, sign))

    def gather_start(h):
        ref = block(h, 0, 0, 0)
        net.put(("x0", h), ref, ref, to_row(1, 0))
        for way in range(2):
            ring_send(h, 1, 0, 1, way)
        ref = block(h, 1, 0, 0)
        net.put(("x1", h, 0), ref, ref, to_row(1, 0))
        for way in range(2):
            ring_send(h, 0, 0, 1, way)

    def gather_mid(h):
        net.wait(("x0", h), block(h, 0, 1, 0), to_row(1, 0))
        for way in range(2):
            ring_send(h, 0, 1, 1, way)

    def gather_step(h, step, n):
        q, dx = streams[n]
        for way in range(2):
            if step <= hops(h, q, dx)[way]:
                sign = 1 - 2 * way
                ref = block(h, q, dx, -sign * step)
                net.wait(("ring", h, q, dx, step, way), ref, to_row(0, -sign))
                ring_send(h, q, dx, step + 1, way)
                if q == 1:
                    net.put(("x1", h, -sign * step), ref, ref, to_row(1, 0))

    def gather_end(h):
        plus, minus = hops(h, 1, 0)
        for dz in range(-plus, minus + 1):
            net.wait(("x1", h, dz), block(h, 1, 1, dz), to_row(1, 0))

    def build(lo, hi):
        def body(t, _):
            slots = cols_ref[t]
            lane = iota((128, 128), 0).astype(jnp.int16)
            total = None
            for n in range(8):
                hit = jnp.broadcast_to(slots[n : n + 1, :], (128, 128)).astype(jnp.int16) == lane
                one = jnp.where(hit, jnp.ones((), BF), jnp.zeros((), BF))
                total = one if total is None else total + one
            at[t] = total
            return 0

        lax.fori_loop(lo, hi, body, 0, unroll=4)

    def multiply(d, h, lo, hi):
        def body(p, last):
            tiles = [at[tab[d, 0, GROUP * p + i]] for i in range(GROUP)]
            sources = [(src, b)[d][h][tab[d, 2, GROUP * p + i]] for i in range(GROUP)]
            key = tab[d, 1, GROUP * p]
            if d == 0:
                left, right = jnp.concatenate(sources, axis=1), jnp.concatenate(tiles, axis=0)
            else:
                left, right = jnp.concatenate(tiles, axis=1), jnp.concatenate(sources, axis=0)
            product = jnp.dot(left, right, preferred_element_type=F32)
            total = jnp.where(key == last, acc[...], 0.0) + product
            acc[...] = total
            s[h][p] = total.astype(BF)
            return key

        first = tab[d, 1, GROUP * (lo - 1)] if lo else jnp.int32(-1)
        lax.fori_loop(lo, hi, body, first, unroll=16)

    def part(d, h, block_id):
        return s[h][tab[d, 3, block_id]].astype(F32)

    def cols_start(h):
        for dx in (1, 0):
            for dy in (1, 3, 2, 0):
                j = dx * 4 + dy
                for k in range(4):
                    snd1[h, j, k] = s[h][tab[0, 3, 4 * col_of(dx, dy, 1) + k]]
                net.put(("core", h, j), snd1.at[h, j], rcv1.at[h, j], to_col(0, 0, 1))

    def cols_second(h):
        for dx in (1, 0):
            for dy in (1, 3, 2, 0):
                j = dx * 4 + dy
                net.wait(("core", h, j), rcv1.at[h, j], to_col(0, 0, 1))
                for k in range(4):
                    rcv1[h, j, k] = (part(0, h, 4 * col_of(dx, dy) + k) + rcv1[h, j, k].astype(F32)).astype(BF)
                if dx == 1:
                    net.put(("qx", h, dy), rcv1.at[h, j, pl.ds(2, 2)], r_qx.at[h, dy], to_col(1, 0))
                if dy:
                    net.put(("py", h, dy, dx), rcv1.at[h, j, pl.ds(0, 2)], r_py.at[h, dy - 1, dx], to_col(0, dy))

    def cols_third(h):
        for dy in (1, 3, 2):
            net.wait(("qx", h, dy), r_qx.at[h, dy], to_col(1, 0))
            r_qx[h, dy] = (rcv1[h, dy, 2:4].astype(F32) + r_qx[h, dy].astype(F32)).astype(BF)
            net.put(("qy", h, dy), r_qx.at[h, dy], r_qy.at[h, dy - 1], to_col(0, dy))
        total = rcv1[h, 4, 0:2].astype(F32)
        for dy in (1, 3, 2):
            net.wait(("py", h, dy, 1), r_py.at[h, dy - 1, 1], to_col(0, 4 - dy))
            total = total + r_py[h, dy - 1, 1].astype(F32)
        snd1[h, 8, 0:2] = total.astype(BF)
        net.put(("px", h), snd1.at[h, 8, pl.ds(0, 2)], r_px.at[h], to_col(1, 0))

    def cols_end(h):
        total = rcv1[h, 0, 0:2].astype(F32)
        for dy in (1, 3, 2):
            net.wait(("py", h, dy, 0), r_py.at[h, dy - 1, 0], to_col(0, 4 - dy))
            total = total + r_py[h, dy - 1, 0].astype(F32)
        net.wait(("px", h), r_px.at[h], to_col(1, 0))
        total = total + r_px[h].astype(F32)
        net.wait(("qx", h, 0), r_qx.at[h, 0], to_col(1, 0))
        second = rcv1[h, 0, 2:4].astype(F32) + r_qx[h, 0].astype(F32)
        for dy in (1, 3, 2):
            net.wait(("qy", h, dy), r_qy.at[h, dy - 1], to_col(0, 4 - dy))
            second = second + r_qy[h, dy - 1].astype(F32)
        for k in range(4):
            value = (total if k < 2 else second)[k % 2]
            mean_t[k, 128 * h : 128 * h + 128, :] = (value / deg_ref[k : k + 1, :].astype(F32)).astype(BF)

    turned_dims = (((1,), (1,)), ((), ()))

    def dense():
        for k in range(4):
            rows = slice(128 * k, 128 * k + 128)
            mean = mean_t[k].astype(F32).T.astype(BF)
            pre = jnp.dot(x_ref[rows, :], sw_ref[...], preferred_element_type=F32)
            pre = pre + jnp.dot(mean, nw_ref[...], preferred_element_type=F32)
            sig = jax.nn.sigmoid(pre)
            out_ref[rows, :] = (pre * sig).astype(BF)
            g = (og_ref[rows, :].astype(F32) * sig * (1.0 + pre * (1.0 - sig))).astype(BF)
            g_ref[k] = g
            d_mean = lax.dot_general(g, nw_ref[...], turned_dims, preferred_element_type=F32)
            divisor = jnp.broadcast_to(deg_ref[k : k + 1, :].astype(F32), (128, 128)).T
            b0[4 * c + k] = (d_mean[:, 0:128] / divisor).astype(BF)
            b1[4 * c + k] = (d_mean[:, 128:256] / divisor).astype(BF)

    def cblock(h, q, dx, dy, dc=0):
        return b[h].at[pl.ds(4 * col_of(dx, dy, dc) + 2 * q, 2)]

    def to_core(h, q, dx, dy):
        ref = cblock(h, q, dx, dy)
        net.put(("bc", h, q, dx, dy), ref, ref, to_col(0, 0, 1))

    def back_start(h):
        ref = cblock(h, 0, 0, 0)
        net.put(("bx0", h), ref, ref, to_col(1, 0))
        ref = cblock(h, 1, 0, 0)
        for dy in (1, 3, 2):
            net.put(("by1", h, dy), ref, ref, to_col(0, dy))
        net.put(("bx1", h, 0), ref, ref, to_col(1, 0))
        ref = cblock(h, 0, 0, 0)
        for dy in (1, 3, 2):
            net.put(("by0", h, 0, dy), ref, ref, to_col(0, dy))
        to_core(h, 0, 0, 0)
        to_core(h, 1, 0, 0)

    def back_mid(h):
        ref = cblock(h, 0, 1, 0)
        net.wait(("bx0", h), ref, to_col(1, 0))
        for dy in (1, 3, 2):
            net.put(("by0", h, 1, dy), ref, ref, to_col(0, dy))
        for dy in (1, 3, 2):
            ref = cblock(h, 1, 0, 4 - dy)
            net.wait(("by1", h, dy), ref, to_col(0, 4 - dy))
            net.put(("bx1", h, dy), ref, ref, to_col(1, 0))
        to_core(h, 0, 1, 0)
        for dy in (1, 3, 2):
            to_core(h, 1, 0, 4 - dy)

    def back_late(h):
        for dy in (1, 3, 2):
            net.wait(("by0", h, 0, dy), cblock(h, 0, 0, 4 - dy), to_col(0, 4 - dy))
            to_core(h, 0, 0, 4 - dy)
        for dy in (0, 1, 3, 2):
            net.wait(("bx1", h, dy), cblock(h, 1, 1, (4 - dy) % 4), to_col(1, 0))
            to_core(h, 1, 1, (4 - dy) % 4)
        for dy in (1, 3, 2):
            net.wait(("by0", h, 1, dy), cblock(h, 0, 1, 4 - dy), to_col(0, 4 - dy))
            to_core(h, 0, 1, 4 - dy)

    def back_end(h):
        for q in range(2):
            for dx in range(2):
                for dy in range(4):
                    net.wait(("bc", h, q, dx, dy), cblock(h, q, dx, dy, 1), to_col(0, 0, 1))

    def rows_start(h):
        rows_first(h, 2)
        rows_first(h, 1)
        for dz in (4, 3, 5, 2, 6, 1, 7, 0):
            for k in range(2):
                t_xa[h, dz, k] = s[h][tab[1, 3, 4 * row_of(1, dz) + 2 + k]]
            net.put(("xa", h, dz), t_xa.at[h, dz], r_xa.at[h, dz], to_row(1, 0))

    def term(h, n, dz):
        q, dx = streams[n]
        dz = dz % 8
        value = [part(1, h, 4 * row_of(dx, dz) + 2 * q + k) for k in range(2)]
        if q == 1:
            value = [value[k] + r_xa[h, dz, k].astype(F32) for k in range(2)]
        return value

    def rows_first(h, n):
        for way in range(2):
            sign = 1 - 2 * way
            far = hops(h, *streams[n])[way]
            if streams[n][0] == 1:
                net.wait(("xa", h, sign * far % 8), r_xa.at[h, sign * far % 8], to_row(1, 0))
            value = term(h, n, sign * far)
            for k in range(2):
                t_z[h, n, way, k] = value[k].astype(BF)
            net.put(("z", h, n, way, 1), t_z.at[h, n, way], r_z.at[h, n, way, 0], to_row(0, sign))

    def rows_second(h):
        rows_first(h, 0)

    def rows_step(h, step, n):
        for way in range(2):
            sign = 1 - 2 * way
            far = hops(h, *streams[n])[way]
            if step >= far:
                continue
            dz = sign * (far - step)
            if streams[n][0] == 1:
                net.wait(("xa", h, dz % 8), r_xa.at[h, dz % 8], to_row(1, 0))
            value = term(h, n, dz)
            ref = r_z.at[h, n, way, step - 1]
            net.wait(("z", h, n, way, step), ref, to_row(0, -sign))
            for k in range(2):
                r_z[h, n, way, step - 1, k] = (value[k] + r_z[h, n, way, step - 1, k].astype(F32)).astype(BF)
            net.put(("z", h, n, way, step + 1), ref, r_z.at[h, n, way, step], to_row(0, sign))

    def rows_sum(h, n):
        if streams[n][0] == 1:
            net.wait(("xa", h, 0), r_xa.at[h, 0], to_row(1, 0))
        value = term(h, n, 0)
        for way in range(2):
            far = hops(h, *streams[n])[way]
            net.wait(("z", h, n, way, far), r_z.at[h, n, way, far - 1], to_row(0, 2 * way - 1))
            value = [value[k] + r_z[h, n, way, far - 1, k].astype(F32) for k in range(2)]
        return value

    def rows_late(h):
        value = rows_sum(h, 2)
        for k in range(2):
            t_xb[h, k] = value[k].astype(BF)
        net.put(("xb", h), t_xb.at[h], r_xb.at[h], to_row(1, 0))

    def own_term(k, h):
        return lax.dot_general(
            g_ref[k], sw_ref[128 * h : 128 * h + 128, :], turned_dims, preferred_element_type=F32
        )

    def rows_end(h):
        lanes = slice(128 * h, 128 * h + 128)
        value = rows_sum(h, 0)
        for k in range(2):
            fg_ref[128 * (k + 2) : 128 * (k + 3), lanes] = (value[k] + own_term(k + 2, h)).astype(BF)
        value = rows_sum(h, 1)
        net.wait(("xb", h), r_xb.at[h], to_row(1, 0))
        for k in range(2):
            back = value[k] + r_xb[h, k].astype(F32)
            fg_ref[128 * k : 128 * (k + 1), lanes] = (back + own_term(k, h)).astype(BF)

    def weights_0():
        for h in range(2):
            rows = slice(128 * h, 128 * h + 128)
            own = jnp.concatenate([src[h][4 * r + k] for k in range(4)], axis=1)
            mean = jnp.concatenate([mean_t[k, rows, :] for k in range(4)], axis=1)
            g = jnp.concatenate([g_ref[k] for k in range(4)], axis=0)
            w_sum[4 * h : 4 * h + 4] = jnp.dot(own, g, preferred_element_type=F32).reshape(4, 32, 256)
            w_sum[8 + 4 * h : 12 + 4 * h] = jnp.dot(mean, g, preferred_element_type=F32).reshape(4, 32, 256)

    def weights_1():
        for d in range(1, 16):
            target = lax.rem(c + d, 16)
            net.put(("w1", d), w_sum.at[target], w_col.at[d - 1], {"col": target})

    def weights_2():
        total = w_sum[c]
        for d in range(1, 16):
            net.wait(("w1", d), w_col.at[d - 1], {"col": lax.rem(c + (16 - d), 16)})
            total = total + w_col[d - 1]
        for n in range(8):
            a, e = n // 2, n % 2
            w_part[n] = total[8 * a : 8 * a + 8, 128 * e : 128 * e + 128]
        w_row[r] = w_part[z]
        for d in range(1, 16):
            target = lax.rem(r + d, 16)
            net.put(("w2", d), w_part.at[lax.rem(target, 8)], w_row.at[r], {"row": target})

    def weights_3():
        for d in range(1, 16):
            source = lax.rem(r + (16 - d), 16)
            net.wait(("w2", d), w_row.at[source], {"row": source})
        total = w_row[0]
        for n in range(1, 16):
            total = total + w_row[n]
        w_z[z] = total
        for dz in range(1, 8):
            net.put(("w3", dz), w_z.at[z], w_z.at[z], to_row(0, dz))

    def weights_4():
        for dz in range(1, 8):
            net.wait(("w3", dz), w_z.at[lax.rem(z + (8 - dz), 8)], to_row(0, 8 - dz))
        for n in range(8):
            a, e = n // 2, n % 2
            w_all[c, 8 * a : 8 * a + 8, 128 * e : 128 * e + 128] = w_z[n]
        for d in range(1, 16):
            net.put(("w4", d), w_all.at[c], w_all.at[c], {"col": lax.rem(c + d, 16)})

    def weights_5():
        for d in range(1, 16):
            source = lax.rem(c + (16 - d), 16)
            net.wait(("w4", d), w_all.at[source], {"col": source})
        for n in range(8):
            sg_ref[32 * n : 32 * n + 32, :] = w_all[n]
            ng_ref[32 * n : 32 * n + 32, :] = w_all[8 + n]

    def wait_cols():
        load_cols.wait()

    gather_start(0)
    wait_cols()
    build(0, 48)
    gather_mid(0)
    build(48, 80)
    gather_step(0, 1, 0)
    build(80, 120)
    gather_step(0, 1, 1)
    build(120, 160)
    gather_step(0, 1, 2)
    build(160, 200)
    gather_step(0, 2, 0)
    build(200, 232)
    gather_start(1)
    gather_step(0, 2, 1)
    build(232, 264)
    gather_step(0, 2, 2)
    build(264, 296)
    gather_step(0, 3, 0)
    build(296, 336)
    gather_mid(1)
    gather_step(0, 3, 1)
    build(336, 376)
    gather_step(0, 3, 2)
    build(376, 416)
    gather_step(1, 1, 0)
    build(416, 432)
    gather_step(1, 1, 1)
    build(432, 448)
    gather_step(1, 1, 2)
    build(448, 464)
    gather_step(0, 4, 0)
    build(464, 496)
    gather_step(0, 4, 1)
    build(496, 512)
    gather_step(0, 4, 2)
    gather_end(0)
    multiply(0, 0, 0, 64)
    gather_step(1, 2, 0)
    gather_step(1, 2, 1)
    gather_step(1, 2, 2)
    multiply(0, 0, 64, 128)
    gather_step(1, 3, 0)
    gather_step(1, 3, 1)
    gather_step(1, 3, 2)
    multiply(0, 0, 128, 176)
    cols_start(0)
    gather_step(1, 4, 0)
    gather_step(1, 4, 1)
    gather_step(1, 4, 2)
    cols_second(0)
    gather_end(1)
    multiply(0, 1, 0, 112)
    cols_third(0)
    multiply(0, 1, 112, 176)
    cols_start(1)
    cols_end(0)
    cols_second(1)
    cols_third(1)
    cols_end(1)
    dense()
    back_start(0)
    weights_0()
    back_mid(0)
    back_late(0)
    back_start(1)
    back_end(0)
    multiply(1, 0, 0, 48)
    back_mid(1)
    multiply(1, 0, 48, 128)
    back_late(1)
    weights_1()
    multiply(1, 0, 128, 176)
    rows_start(0)
    back_end(1)
    multiply(1, 1, 0, 96)
    rows_second(0)
    rows_step(0, 1, 2)
    rows_step(0, 1, 1)
    multiply(1, 1, 96, 176)
    weights_2()
    rows_start(1)
    rows_step(0, 1, 0)
    rows_step(0, 2, 2)
    rows_step(0, 2, 1)
    rows_second(1)
    rows_step(0, 2, 0)
    weights_3()
    rows_step(1, 1, 2)
    rows_step(0, 3, 2)
    rows_step(1, 1, 1)
    rows_step(0, 3, 1)
    rows_step(1, 1, 0)
    weights_4()
    rows_step(0, 3, 0)
    rows_step(1, 2, 2)
    rows_step(1, 2, 1)
    rows_late(0)
    rows_step(1, 2, 0)
    rows_step(1, 3, 2)
    rows_step(1, 3, 1)
    rows_step(1, 3, 0)
    rows_end(0)
    rows_late(1)
    weights_5()
    rows_end(1)
    net.finish()


def hand_on(*refs):
    for n in range(4):
        refs[4 + n][...] = refs[n][...]


def shards(features, self_weight, neigh_weight, tile_coords, tile_columns, degree, out_grad):
    vmem = pl.BlockSpec(memory_space=pltpu.VMEM)
    shape = jax.ShapeDtypeStruct
    tab = pl.pallas_call(order_tiles, out_shape=shape((2, 8, LANES), jnp.int32))(tile_coords.reshape(TILES, 2).T)
    results = pl.pallas_call(
        main_kernel,
        out_shape=(shape((512, 256), BF), shape((512, 256), BF), shape((256, 256), F32), shape((256, 256), F32)),
        in_specs=[pl.BlockSpec(memory_space=pltpu.SMEM)] + [vmem] * 3 + [pl.BlockSpec(memory_space=pl.ANY)] + [vmem] * 2,
        out_specs=[vmem] * 4,
        scratch_shapes=[
            pltpu.VMEM((TILES + 1, 128, 128), BF),
            pltpu.VMEM((64, 128, 128), BF),
            pltpu.VMEM((64, 128, 128), BF),
            pltpu.VMEM((GROUPS + 1, 128, 128), BF),
            pltpu.VMEM((GROUPS + 1, 128, 128), BF),
            pltpu.VMEM((128, 128), F32),
            pltpu.VMEM((64, 128, 128), BF),
            pltpu.VMEM((64, 128, 128), BF),
            pltpu.VMEM((4, 256, 128), BF),
            pltpu.VMEM((4, 128, 256), BF),
            pltpu.VMEM((2, 9, 4, 128, 128), BF),
            pltpu.VMEM((2, 8, 4, 128, 128), BF),
            pltpu.VMEM((2, 3, 2, 2, 128, 128), BF),
            pltpu.VMEM((2, 2, 128, 128), BF),
            pltpu.VMEM((2, 4, 2, 128, 128), BF),
            pltpu.VMEM((2, 3, 2, 128, 128), BF),
            pltpu.VMEM((2, 8, 2, 128, 128), BF),
            pltpu.VMEM((2, 8, 2, 128, 128), BF),
            pltpu.VMEM((2, 3, 2, 4, 2, 128, 128), BF),
            pltpu.VMEM((2, 3, 2, 2, 128, 128), BF),
            pltpu.VMEM((2, 2, 128, 128), BF),
            pltpu.VMEM((2, 2, 128, 128), BF),
            pltpu.VMEM((16, 32, 256), F32),
            pltpu.VMEM((15, 32, 256), F32),
            pltpu.VMEM((8, 8, 128), F32),
            pltpu.VMEM((16, 8, 128), F32),
            pltpu.VMEM((8, 8, 128), F32),
            pltpu.VMEM((16, 32, 256), F32),
            pltpu.VMEM((TILES, 8, 128), jnp.int32),
            pltpu.SemaphoreType.DMA((1,)),
            pltpu.SemaphoreType.DMA((N_SEMS,)),
            pltpu.SemaphoreType.DMA((N_SEMS,)),
        ],
        compiler_params=pltpu.CompilerParams(
            collective_id=0, has_side_effects=True, vmem_limit_bytes=60 * 1024 * 1024
        ),
    )(
        tab,
        features,
        self_weight,
        neigh_weight,
        tile_columns.reshape(TILES, 8, 128),
        degree.reshape(4, 128),
        out_grad,
    )
    return pl.pallas_call(hand_on, out_shape=tuple(shape(a.shape, a.dtype) for a in results))(*results)


def solution(mesh):
    return jax.shard_map(
        shards,
        mesh=mesh,
        in_specs=(
            P(("row", "col"), None),
            P(),
            P(),
            P("row", "col", None, None),
            P("row", "col", None, None, None),
            P(("row", "col")),
            P(("row", "col"), None),
        ),
        out_specs=(P(("row", "col"), None), P(("row", "col"), None), P(), P()),
        check_vma=False,
    )
```
